32 devices in a mesh: row: 8 (over z, core), col: 4 (over y, x).
Axes of the slice: x: 2, y: 2, z: 4, core: 2. Of those that a mesh axis runs over, the one named last changes fastest.
Arguments:
- tokens: bfloat16 [1024, 6144], P('col', 'row'), may hold values from -6 to 6
- up_latent: bfloat16 [6144, 24576], P('row', 'col'), may hold values from -1.0206207 to 1.0206207
- down_latent: bfloat16 [24576, 6144], P('col', 'row'), may hold values from -0.51031036 to 0.51031036
- out_grad: bfloat16 [1024, 6144], P('col', 'row'), may hold values from -6 to 6
Outputs:
- output: bfloat16 [1024, 6144], P('col', 'row')
- in_grad: bfloat16 [1024, 6144], P('col', 'row')
- up_grad: bfloat16 [6144, 24576], P('row', 'col')
- down_grad: bfloat16 [24576, 6144], P('col', 'row')
The draws below stay inside these ranges and needn't reach their ends.
All inputs are finite; a program needn't handle non-finite values.
Results may differ from the reference program's by a relative error of at most 0.028.
Values may be sent and summed in bfloat16 or wider, within the bound.
A program may use at most 128 MiB of HBM per device.

```python
import math
import jax
import jax.numpy as jnp
from jax import lax

D = 6144
FFW = 24576
TOKENS = 1024
N_ROW = 8
N_COL = 4


def latent_matrix(key, row_total, col_total, fan_in):
    key_rows, key_cols, key_base = jax.random.split(key, 3)
    trend = 3.0 ** (jnp.arange(row_total, dtype=jnp.float32) / max(row_total - 1, 1))
    row_scale = 10.0 ** (0.5 * jax.random.uniform(key_rows, (row_total, 1), jnp.float32)) * trend[:, None]
    col_scale = 10.0 ** (0.5 * jax.random.uniform(key_cols, (1, col_total), jnp.float32))
    base = jnp.clip(jax.random.normal(key_base, (row_total, col_total), jnp.float32), -4.0, 4.0)
    limit = 79.0 * fan_in ** (-0.5)
    values = jnp.clip(base * row_scale * col_scale * (0.5 * fan_in ** (-0.5)), -limit, limit)
    return values.astype(jnp.bfloat16)


def draw_up_latent(key, part):
    return latent_matrix(jax.random.fold_in(key, 11), D, FFW, D)


def draw_down_latent(key, part):
    return latent_matrix(jax.random.fold_in(key, 23), FFW, D, FFW)


def levels(own_key, extent, pieces, least, high):
    def one(axis_at, parts):
        draws = jax.random.uniform(jax.random.fold_in(jax.random.fold_in(own_key, 6), axis_at), (parts,), jnp.float32, least / len(pieces), high / len(pieces))
        return jnp.repeat(jnp.exp(draws), extent[axis_at] // parts).reshape((-1,) + (1,) * (len(extent) - axis_at - 1))

    loudness = one(*pieces[0])
    for cut in pieces[1:]:
        loudness = loudness * one(*cut)
    return loudness


def bell_draw(own_key, extent, deviation, bound, cuts=(), kind=jnp.bfloat16):
    level = levels(own_key, extent, cuts, -0.22, 0.18) if cuts else 1.0
    result = jax.random.normal(own_key, extent, jnp.float32) * deviation * level
    return jnp.minimum(jnp.maximum(result, -bound), bound).astype(kind)


def setup_inputs(seed: int = 0) -> dict:
    key_of = jax.random.split(jax.random.key(seed), 5)
    return {
        "tokens": bell_draw(key_of[0], (TOKENS, D), 1.0, 6.0, ((0, 4), (1, 8))),
        "up_latent": draw_up_latent(jax.random.fold_in(key_of[4], 71), 0),
        "down_latent": draw_down_latent(jax.random.fold_in(key_of[4], 71), 0),
        "out_grad": bell_draw(key_of[3], (TOKENS, D), 1.0, 6.0, ((0, 4), (1, 8))),
    }


gelu_coef = math.sqrt(2.0 / math.pi)

def gelu_value(values):
    tanh_arg = gelu_coef * (values + 0.044715 * values * values * values)
    return 0.5 * values * (1.0 + jnp.tanh(tanh_arg))

def gelu_slope(values):
    tanh_val = jnp.tanh(gelu_coef * (values + 0.044715 * values * values * values))
    return 0.5 * (1.0 + tanh_val) + 0.5 * values * (1.0 - tanh_val * tanh_val) * gelu_coef * (1.0 + 3.0 * 0.044715 * values * values)

def ternary(latent, fan_in):
    limit = 0.8 * fan_in ** (-0.5)
    wide = latent.astype(jnp.float32)
    upper = jnp.where(wide > limit, 1.0, 0.0)
    lower = jnp.where(wide < -limit, 1.0, 0.0)
    return (upper - lower).astype(jnp.bfloat16)

def rounded(values):
    return lax.optimization_barrier(values.astype(jnp.bfloat16)).astype(jnp.float32)

def blocked_sum(left, right, count, scale, transposed):
    width = left.shape[1] // count
    total = None
    for index in range(count):
        left_block = left[:, index * width:(index + 1) * width]
        if transposed:
            right_block = right[:, index * width:(index + 1) * width].T
        else:
            right_block = right[index * width:(index + 1) * width, :]
        partial_sum = scale * jnp.dot(left_block, right_block, preferred_element_type=jnp.float32)
        term = rounded(partial_sum)
        total = term if total is None else total + term
    return total

def reference(tokens, up_latent, down_latent, out_grad):
    up_scale = jnp.sum(jnp.abs(up_latent.astype(jnp.float32))) / (D * FFW)
    down_scale = jnp.sum(jnp.abs(down_latent.astype(jnp.float32))) / (D * FFW)
    up_tern = ternary(up_latent, D)
    down_tern = ternary(down_latent, FFW)
    grad_norm = 1.0 / math.sqrt(TOKENS)
    hidden = blocked_sum(tokens, up_tern, N_ROW, up_scale, False)
    act = gelu_value(hidden).astype(jnp.bfloat16)
    output = blocked_sum(act, down_tern, N_COL, down_scale, False).astype(jnp.bfloat16)
    down_grad = (jnp.dot(act.T, out_grad, preferred_element_type=jnp.float32) * grad_norm).astype(jnp.bfloat16)
    act_grad = blocked_sum(out_grad, down_tern, N_ROW, down_scale, True)
    hidden_grad = (act_grad * gelu_slope(hidden)).astype(jnp.bfloat16)
    up_grad = (jnp.dot(tokens.T, hidden_grad, preferred_element_type=jnp.float32) * grad_norm).astype(jnp.bfloat16)
    in_grad = blocked_sum(hidden_grad, up_tern, N_COL, up_scale, True).astype(jnp.bfloat16)
    return (output, in_grad, up_grad, down_grad)
```

```python
import math

import jax
import jax.numpy as jnp
from jax import lax
from jax.sharding import PartitionSpec as P

gelu_coef = math.sqrt(2.0 / math.pi)
in_flight = 2


def gelu_both(values):
    tanh_val = jnp.tanh(gelu_coef * (values + 0.044715 * values * values * values))
    value = 0.5 * values * (1.0 + tanh_val)
    slope = 0.5 * (1.0 + tanh_val) + 0.5 * values * (1.0 - tanh_val * tanh_val) * gelu_coef * (
        1.0 + 3.0 * 0.044715 * values * values
    )
    return value, slope


def ternary(latent, fan_in):
    limit = 0.8 * fan_in ** (-0.5)
    wide = latent.astype(jnp.float32)
    upper = jnp.where(wide > limit, 1.0, 0.0)
    lower = jnp.where(wide < -limit, 1.0, 0.0)
    return (upper - lower).astype(jnp.bfloat16)


def dot(left, right, left_dim, right_dim):
    return lax.dot_general(
        left, right, (((left_dim,), (right_dim,)), ((), ())), preferred_element_type=jnp.float32
    )


def body(tokens, up_latent, down_latent, out_grad):
    f32, bf16 = jnp.float32, jnp.bfloat16
    rows_axis = lax.axis_size("row")
    cols_axis = lax.axis_size("col")
    chips = rows_axis // 2
    block = tokens.shape[0]
    half = block // 2
    hid = up_latent.shape[1]
    cuts = max(1, 8 // cols_axis)
    width = hid // cuts
    grad_norm = 1.0 / math.sqrt(block * cols_axis)
    core = lax.rem(lax.axis_index("row"), 2)

    def partner(values):
        return lax.ppermute(values, "row", [(i, i ^ 1) for i in range(rows_axis)])

    def across(values, shift):
        if shift == 0:
            return values
        return lax.ppermute(values, "col", [(i, i ^ shift) for i in range(cols_axis)])

    def line(values, step):
        pairs = []
        for c in range(2):
            pairs.append((2 * step + c, 2 * step + 2 + c))
            last = chips - 1 - step
            pairs.append((2 * last + c, 2 * last - 2 + c))
        return lax.ppermute(values, "row", pairs)

    def own_first(values):
        return jnp.where(core == 0, values, jnp.concatenate([values[half:], values[:half]], axis=0))

    entry_total = up_latent.size * rows_axis * cols_axis
    scale_sums = lax.psum(
        (
            jnp.sum(jnp.abs(up_latent.astype(f32))),
            jnp.sum(jnp.abs(down_latent.astype(f32))),
        ),
        ("row", "col"),
    )
    up_scale = scale_sums[0] / entry_total
    down_scale = scale_sums[1] / entry_total
    up_fan = up_latent.shape[0] * rows_axis
    down_fan = hid * cols_axis
    up_tern = [ternary(up_latent[:, a * width : (a + 1) * width], up_fan) for a in range(cuts)]
    down_tern = [ternary(down_latent[a * width : (a + 1) * width], down_fan) for a in range(cuts)]

    tok = [own_first(across(tokens, j)) for j in range(cols_axis)]
    grad = [own_first(across(out_grad, j)) for j in range(cols_axis)]

    gate = []

    def row_sum(partial):
        own = partial[:half].astype(f32)
        base = (own + partner(partial[half:].astype(bf16)).astype(f32)).astype(bf16)
        if len(gate) >= in_flight:
            base, _ = lax.optimization_barrier((base, gate[-in_flight]))
        total = base.astype(f32)
        message = base
        for step in range(chips - 1):
            got = line(message, step)
            if step == 0:
                gate.append(got)
            total = total + got.astype(f32)
            message = (base.astype(f32) + got.astype(f32)).astype(bf16)
        return total

    order = [(j, a) for j in range(cols_axis) for a in range(cuts)]
    act, slope = {}, {}
    for j, a in order:
        hidden = up_scale * row_sum(dot(tok[j], up_tern[a], 1, 0))
        value, slope_f32 = gelu_both(hidden)
        value = value.astype(bf16)
        slope[j, a] = slope_f32.astype(bf16)
        act[j, a] = jnp.concatenate([value, partner(value)], axis=0)

    def to_owner(parts_of, weights, dim, scale):
        total = None
        for j in range(cols_axis):
            part = sum(dot(parts_of[j, a], weights[a], 1, dim) for a in range(cuts))
            part = across(own_first((scale * part).astype(bf16)), j).astype(f32)
            total = part if total is None else total + part
        return total.astype(bf16)

    grad_panel = jnp.concatenate(grad, axis=0)
    tok_panel = jnp.concatenate(tok, axis=0)
    output = to_owner(act, down_tern, 0, down_scale)
    down_grad = jnp.concatenate(
        [
            (
                dot(jnp.concatenate([act[j, a] for j in range(cols_axis)], axis=0), grad_panel, 0, 0)
                * grad_norm
            ).astype(bf16)
            for a in range(cuts)
        ],
        axis=0,
    )

    hidden_grad = {}
    for j in reversed(range(cols_axis)):
        for a in range(cuts):
            act_grad = down_scale * row_sum(dot(grad[j], down_tern[a], 1, 1))
            value = (act_grad * slope[j, a].astype(f32)).astype(bf16)
            hidden_grad[j, a] = jnp.concatenate([value, partner(value)], axis=0)
    in_grad = to_owner(hidden_grad, up_tern, 1, up_scale)
    up_grad = jnp.concatenate(
        [
            (
                dot(
                    tok_panel,
                    jnp.concatenate([hidden_grad[j, a] for j in range(cols_axis)], axis=0),
                    0,
                    0,
                )
                * grad_norm
            ).astype(bf16)
            for a in range(cuts)
        ],
        axis=1,
    )
    return (output, in_grad, up_grad, down_grad)


def solution(mesh):
    in_specs = (P("col", "row"), P("row", "col"), P("col", "row"), P("col", "row"))
    out_specs = (P("col", "row"), P("col", "row"), P("row", "col"), P("col", "row"))
    return jax.shard_map(body, mesh=mesh, in_specs=in_specs, out_specs=out_specs, check_vma=False)
```

```python
import functools
import math

import jax
import jax.numpy as jnp
from jax import lax
from jax.experimental import pallas as pl
from jax.experimental.pallas import tpu as pltpu
from jax.sharding import PartitionSpec as P

gelu_coef = math.sqrt(2.0 / math.pi)
f32, bf16 = jnp.float32, jnp.bfloat16
x_depth = 4
act_depth = 4


def gelu_both(values):
    square = values * values
    tanh_val = jnp.tanh(gelu_coef * (values + 0.044715 * square * values))
    value = 0.5 * values * (1.0 + tanh_val)
    slope = 0.5 * (1.0 + tanh_val) + 0.5 * values * (1.0 - tanh_val * tanh_val) * gelu_coef * (
        1.0 + 3.0 * 0.044715 * square
    )
    return value, slope


def ternary(latent, limit):
    wide = latent.astype(f32)
    upper = jnp.where(wide > limit, 1.0, 0.0)
    lower = jnp.where(wide < -limit, 1.0, 0.0)
    return (upper - lower).astype(bf16)


def dot(left, right, left_dim, right_dim):
    return lax.dot_general(
        left, right, (((left_dim,), (right_dim,)), ((), ())), preferred_element_type=f32
    )


def kernel(
    rows, cols, width, depth,
    tokens, up_lat, down_lat, out_grad,
    output, in_grad, up_grad, down_grad,
    tok, grad, tok_t, sums, sums_col, sums_row, base, from_left, from_right, to_right, to_left,
    x_send, x_recv, act, slope, total_out, wide_up, wide_down, act_t, down_stage, up_stage,
    part_send, part_recv,
    tok_ss, tok_rs, grad_ss, grad_rs, sc_ss, sc_rs, sr_ss, sr_rs,
    right_ss, left_rs, left_ss, right_rs, x_ss, x_rs, a_ss, a_rs, part_ss, part_rs,
    down_sem, up_sem, credit_right, credit_left, credit_x, credit_a,
):
    chips = rows // 2
    block, model = tokens.shape
    total = block * cols
    half = total // 2
    hid = up_lat.shape[1]
    cuts = hid // width
    count = 2 * cuts
    tile = 256 if model % 256 == 0 else 128
    up_limit = 0.8 * (model * rows) ** (-0.5)
    down_limit = 0.8 * (hid * cols) ** (-0.5)
    grad_norm = 1.0 / math.sqrt(total)
    me_row, me_col = lax.axis_index("row"), lax.axis_index("col")
    core = lax.rem(me_row, 2)
    z = lax.div(me_row, 2)
    mate = me_row + 1 - 2 * core
    right, left = me_row + 2, me_row - 2
    mine = pl.ds(pl.multiple_of(core * half, half), half)
    other = pl.ds(pl.multiple_of((1 - core) * half, half), half)

    def send(src, dst, send_sem, recv_sem, **where):
        return pltpu.make_async_remote_copy(
            src_ref=src, dst_ref=dst, send_sem=send_sem, recv_sem=recv_sem,
            device_id=where, device_id_type=pl.DeviceIdType.MESH,
        )

    def peer_col(k):
        return lax.rem(me_col + k, cols)

    def peer_row(k):
        return lax.rem(me_row + k, rows)

    barrier = pltpu.get_barrier_semaphore()
    for k in range(1, cols):
        pl.semaphore_signal(barrier, 1, device_id={"col": peer_col(k)}, device_id_type=pl.DeviceIdType.MESH)
    for k in range(1, rows):
        pl.semaphore_signal(barrier, 1, device_id={"row": peer_row(k)}, device_id_type=pl.DeviceIdType.MESH)
    pl.semaphore_wait(barrier, cols + rows - 2)

    own_block = pl.ds(pl.multiple_of(me_col * block, block), block)

    def panel_copy(src, panel, ss, rs, k):
        return send(src, panel.at[own_block], ss.at[k], rs.at[k], col=peer_col(k))

    for k in range(1, cols):
        panel_copy(tokens, tok, tok_ss, tok_rs, k).start()
    for k in range(1, cols):
        panel_copy(out_grad, grad, grad_ss, grad_rs, k).start()
    tok[own_block] = tokens[...]
    grad[own_block] = out_grad[...]

    def magnitudes(ref, step):
        def add(i, acc):
            piece = jnp.abs(ref[pl.ds(pl.multiple_of(i * step, step), step), :].astype(f32))
            return acc + jnp.sum(piece.reshape(step // 8, 8, piece.shape[1]), axis=0)

        acc = lax.fori_loop(0, ref.shape[0] // step, add, jnp.zeros((8, ref.shape[1]), f32))
        return sum(acc[:, k * 128 : (k + 1) * 128] for k in range(ref.shape[1] // 128))

    sums[0] = magnitudes(up_lat, 16)
    sums[1] = magnitudes(down_lat, 64)

    def exchange(slots, ss, rs, n, target):
        for k in range(1, n):
            send(sums, slots.at[k], ss.at[k], rs.at[k], **target(k)).start()
        for k in range(1, n):
            send(sums, slots.at[k], ss.at[k], rs.at[k], **target(k)).wait()
        whole = sums[...]
        for k in range(1, n):
            whole = whole + slots[k]
        sums[...] = whole

    exchange(sums_col, sc_ss, sc_rs, cols, lambda k: {"col": peer_col(k)})
    exchange(sums_row, sr_ss, sr_rs, rows, lambda k: {"row": peer_row(k)})
    entries = float(up_lat.shape[0] * up_lat.shape[1] * rows * cols)
    up_scale = jnp.sum(sums[0]) / entries
    down_scale = jnp.sum(sums[1]) / entries

    @pl.when(z == 0)
    def _():
        from_left[...] = jnp.zeros_like(from_left)

    @pl.when(z == chips - 1)
    def _():
        from_right[...] = jnp.zeros_like(from_right)

    for k in range(1, cols):
        panel_copy(tokens, tok, tok_ss, tok_rs, k).wait()
    for k in range(cols):
        tok_t[:, k * block : (k + 1) * block] = tok[k * block : (k + 1) * block, :].T

    def right_copy(c):
        return send(to_right.at[lax.rem(c, 2)], from_left.at[lax.rem(c, depth)],
                    right_ss.at[lax.rem(c, 2)], left_rs.at[lax.rem(c, depth)], row=right)

    def left_copy(c):
        return send(to_left.at[lax.rem(c, 2)], from_right.at[lax.rem(c, depth)],
                    left_ss.at[lax.rem(c, 2)], right_rs.at[lax.rem(c, depth)], row=left)

    def x_copy(c):
        return send(x_send.at[lax.rem(c, 2)], x_recv.at[lax.rem(c, x_depth)],
                    x_ss.at[lax.rem(c, 2)], x_rs.at[lax.rem(c, x_depth)], row=mate)

    def act_copy(c):
        place = act.at[lax.rem(c, act_depth), mine]
        return send(place, place, a_ss.at[lax.rem(c, act_depth)], a_rs.at[lax.rem(c, act_depth)], row=mate)

    def part_copy(which, k):
        rows_of = pl.ds(pl.multiple_of(peer_col(k) * block, block), block)
        return send(part_send.at[which, rows_of], part_recv.at[which, k],
                    part_ss.at[which, k], part_rs.at[which, k], col=peer_col(k))

    def chunk_of(c):
        return pl.ds(pl.multiple_of(c * width, width), width)

    def down_copy(c):
        return pltpu.make_async_copy(down_stage.at[lax.rem(c, 2)], down_grad.at[chunk_of(c)], down_sem.at[lax.rem(c, 2)])

    def up_copy(c):
        return pltpu.make_async_copy(up_stage.at[lax.rem(c, 2)], up_grad.at[:, chunk_of(c)], up_sem.at[lax.rem(c, 2)])

    def valid(c):
        return (c >= 0) & (c < count)

    def credit(sem, device):
        pl.semaphore_signal(sem, 1, device_id={"row": device}, device_id_type=pl.DeviceIdType.MESH)

    def partial(c, left_ref, wide, right_dim):
        slot = lax.rem(c, depth)

        @pl.loop(0, half // block)
        def _(r):
            at = pl.multiple_of(r * block, block)
            own_rows = left_ref[pl.ds(pl.multiple_of(core * half + at, block), block), :]
            base[slot, pl.ds(at, block), :] = dot(own_rows, wide[...], 1, right_dim).astype(bf16)
            mate_rows = left_ref[pl.ds(pl.multiple_of((1 - core) * half + at, block), block), :]
            x_send[lax.rem(c, 2), pl.ds(at, block), :] = dot(mate_rows, wide[...], 1, right_dim).astype(bf16)

    def accumulate(c, first, wide, right_dim):
        slot = lax.rem(c, act_depth)

        @pl.when(first)
        def _():
            @pl.loop(0, cols)
            def _(r):
                at = pl.ds(pl.multiple_of(r * block, block), block)
                total_out[at, :] = dot(act[slot, at, :], wide[...], 1, right_dim)

        @pl.when(jnp.logical_not(first))
        def _():
            @pl.loop(0, cols)
            def _(r):
                at = pl.ds(pl.multiple_of(r * block, block), block)
                total_out[at, :] += dot(act[slot, at, :], wide[...], 1, right_dim)

    def finish(which, scale):
        @pl.loop(0, cols)
        def _(r):
            at = pl.ds(pl.multiple_of(r * block, block), block)
            part_send[which, at, :] = (scale * total_out[at, :]).astype(bf16)

        for k in range(1, cols):
            part_copy(which, k).start()

    def step(i, carry):
        s = i - 1
        c_right = s - 2 - 2 * z
        c_left = s - 2 - 2 * (chips - 1 - z)
        c_act = s - 2 * chips
        has_right, has_left = z < chips - 1, z > 0

        @pl.when(valid(c_right) & has_right)
        def _():
            @pl.when(c_right >= depth)
            def _():
                pl.semaphore_wait(credit_right, 1)

            right_copy(c_right).start()

        @pl.when(valid(c_left) & has_left)
        def _():
            @pl.when(c_left >= depth)
            def _():
                pl.semaphore_wait(credit_left, 1)

            left_copy(c_left).start()

        @pl.when(valid(s))
        def _():
            @pl.when(s >= x_depth)
            def _():
                pl.semaphore_wait(credit_x, 1)

            x_copy(s).start()

        @pl.when(valid(c_act))
        def _():
            @pl.when(c_act >= act_depth)
            def _():
                pl.semaphore_wait(credit_a, 1)

            act_copy(c_act).start()

        c = s + 1

        @pl.when((s >= 1) & (s - 1 < count))
        def _():
            x_copy(s - 1).wait_send()

        @pl.when(c < cuts)
        def _():
            wide_up[...] = ternary(up_lat[:, chunk_of(c)], up_limit)
            partial(c, tok, wide_up, 0)

        @pl.when(s == min(2, cuts - 1))
        def _():
            for k in range(1, cols):
                panel_copy(out_grad, grad, grad_ss, grad_rs, k).wait()

        @pl.when((c >= cuts) & (c < count))
        def _():
            wide_down[...] = ternary(down_lat[chunk_of(c - cuts), :], down_limit)
            partial(c, grad, wide_down, 1)

        c_mul = s - 2 * chips - 1

        @pl.when(valid(c_mul))
        def _():
            act_copy(c_mul).wait()
            slot = lax.rem(c_mul, act_depth)

            @pl.when(c_mul < cuts)
            def _():
                wide_down[...] = ternary(down_lat[chunk_of(c_mul), :], down_limit)
                accumulate(c_mul, c_mul == 0, wide_down, 0)

                @pl.when(c_mul >= 2)
                def _():
                    down_copy(c_mul - 2).wait()

                @pl.loop(0, cols)
                def _(r):
                    at = pl.ds(pl.multiple_of(r * block, block), block)
                    act_t[:, at] = act[slot, at, :].T

                @pl.loop(0, model // tile)
                def _(r):
                    at = pl.ds(pl.multiple_of(r * tile, tile), tile)
                    down_stage[lax.rem(c_mul, 2), :, at] = (dot(act_t[...], grad[:, at], 1, 0) * grad_norm).astype(bf16)

                down_copy(c_mul).start()

            @pl.when(c_mul == cuts - 1)
            def _():
                finish(0, down_scale)

            @pl.when(c_mul >= cuts)
            def _():
                c_up = c_mul - cuts
                wide_up[...] = ternary(up_lat[:, chunk_of(c_up)], up_limit)
                accumulate(c_mul, c_up == 0, wide_up, 1)

                @pl.when(c_up >= 2)
                def _():
                    up_copy(c_up - 2).wait()

                @pl.loop(0, model // tile)
                def _(r):
                    at = pl.ds(pl.multiple_of(r * tile, tile), tile)
                    up_stage[lax.rem(c_up, 2), at, :] = (dot(tok_t[at, :], act[slot], 1, 0) * grad_norm).astype(bf16)

                up_copy(c_up).start()

            @pl.when(c_mul == count - 1)
            def _():
                finish(1, up_scale)

            @pl.when(c_mul + act_depth < count)
            def _():
                credit(credit_a, mate)

        @pl.when(valid(c_right - 1) & has_right)
        def _():
            right_copy(c_right - 1).wait_send()

        @pl.when(valid(c_left - 1) & has_left)
        def _():
            left_copy(c_left - 1).wait_send()

        c_base = s - 1

        @pl.when(valid(c_base))
        def _():
            x_copy(c_base).wait_recv()
            slot = lax.rem(c_base, depth)
            both = (base[slot].astype(f32) + x_recv[lax.rem(c_base, x_depth)].astype(f32)).astype(bf16)
            base[slot] = both

            @pl.when(z == 0)
            def _():
                to_right[lax.rem(c_base, 2)] = both

            @pl.when(z == chips - 1)
            def _():
                to_left[lax.rem(c_base, 2)] = both

            @pl.when(c_base + x_depth < count)
            def _():
                credit(credit_x, mate)

        c_from_left = s - 1 - 2 * z

        @pl.when(valid(c_from_left) & has_left)
        def _():
            right_copy(c_from_left).wait_recv()

            @pl.when(has_right)
            def _():
                slot = lax.rem(c_from_left, depth)
                to_right[lax.rem(c_from_left, 2)] = (
                    base[slot].astype(f32) + from_left[slot].astype(f32)
                ).astype(bf16)

        c_from_right = s - 1 - 2 * (chips - 1 - z)

        @pl.when(valid(c_from_right) & has_right)
        def _():
            left_copy(c_from_right).wait_recv()

            @pl.when(has_left)
            def _():
                slot = lax.rem(c_from_right, depth)
                to_left[lax.rem(c_from_right, 2)] = (
                    base[slot].astype(f32) + from_right[slot].astype(f32)
                ).astype(bf16)

        c_sum = s - (2 * chips - 1)

        @pl.when(valid(c_sum))
        def _():
            slot = lax.rem(c_sum, depth)
            aslot = lax.rem(c_sum, act_depth)

            @pl.loop(0, half // 64)
            def _(r):
                at = pl.ds(pl.multiple_of(r * 64, 64), 64)
                out_at = pl.ds(pl.multiple_of(core * half + r * 64, 64), 64)
                whole = (
                    base[slot, at, :].astype(f32)
                    + from_left[slot, at, :].astype(f32)
                    + from_right[slot, at, :].astype(f32)
                )

                @pl.when(c_sum < cuts)
                def _():
                    value, slope_value = gelu_both(up_scale * whole)
                    act[aslot, out_at, :] = value.astype(bf16)
                    slope[c_sum, at, :] = slope_value.astype(bf16)

                @pl.when(c_sum >= cuts)
                def _():
                    act[aslot, out_at, :] = (
                        down_scale * whole * slope[c_sum - cuts, at, :].astype(f32)
                    ).astype(bf16)

            @pl.when((c_sum + depth < count) & has_left)
            def _():
                credit(credit_right, left)

            @pl.when((c_sum + depth < count) & has_right)
            def _():
                credit(credit_left, right)

        return carry

    lax.fori_loop(0, count + 2 * chips + 2, step, 0)

    for c in range(max(0, cuts - 2), cuts):
        down_copy(c).wait()
        up_copy(c).wait()
    for which, scale, out in ((0, down_scale, output), (1, up_scale, in_grad)):
        for k in range(1, cols):
            part_copy(which, k).wait()
        result = part_send[which, own_block, :].astype(f32)
        for k in range(1, cols):
            result = result + part_recv[which, k].astype(f32)
        out[...] = result.astype(bf16)


def body(tokens, up_latent, down_latent, out_grad):
    rows, cols = lax.axis_size("row"), lax.axis_size("col")
    block, model = tokens.shape
    total, hid = block * cols, up_latent.shape[1]
    half = total // 2
    width = 256
    depth = rows + 1
    cuts = hid // width
    vmem = pl.BlockSpec(memory_space=pltpu.VMEM)
    anywhere = pl.BlockSpec(memory_space=pl.ANY)
    dma = pltpu.SemaphoreType.DMA
    scratch = [
        pltpu.VMEM((total, model), bf16),
        pltpu.VMEM((total, model), bf16),
        pltpu.VMEM((model, total), bf16),
        pltpu.VMEM((2, 8, 128), f32),
        pltpu.VMEM((cols, 2, 8, 128), f32),
        pltpu.VMEM((rows, 2, 8, 128), f32),
        pltpu.VMEM((depth, half, width), bf16),
        pltpu.VMEM((depth, half, width), bf16),
        pltpu.VMEM((depth, half, width), bf16),
        pltpu.VMEM((2, half, width), bf16),
        pltpu.VMEM((2, half, width), bf16),
        pltpu.VMEM((2, half, width), bf16),
        pltpu.VMEM((x_depth, half, width), bf16),
        pltpu.VMEM((act_depth, total, width), bf16),
        pltpu.VMEM((cuts, half, width), bf16),
        pltpu.VMEM((total, model), f32),
        pltpu.VMEM((model, width), bf16),
        pltpu.VMEM((width, model), bf16),
        pltpu.VMEM((width, total), bf16),
        pltpu.VMEM((2, width, model), bf16),
        pltpu.VMEM((2, model, width), bf16),
        pltpu.VMEM((2, total, model), bf16),
        pltpu.VMEM((2, cols, block, model), bf16),
        dma((cols,)), dma((cols,)), dma((cols,)), dma((cols,)),
        dma((cols,)), dma((cols,)), dma((rows,)), dma((rows,)),
        dma((2,)), dma((depth,)), dma((2,)), dma((depth,)),
        dma((2,)), dma((x_depth,)), dma((act_depth,)), dma((act_depth,)),
        dma((2, cols)), dma((2, cols)),
        dma((2,)), dma((2,)),
        pltpu.SemaphoreType.REGULAR,
        pltpu.SemaphoreType.REGULAR,
        pltpu.SemaphoreType.REGULAR,
        pltpu.SemaphoreType.REGULAR,
    ]
    return pl.pallas_call(
        functools.partial(kernel, rows, cols, width, depth),
        out_shape=(
            jax.ShapeDtypeStruct(tokens.shape, bf16),
            jax.ShapeDtypeStruct(tokens.shape, bf16),
            jax.ShapeDtypeStruct(up_latent.shape, bf16),
            jax.ShapeDtypeStruct(down_latent.shape, bf16),
        ),
        in_specs=[vmem] * 4,
        out_specs=(vmem, vmem, anywhere, anywhere),
        scratch_shapes=scratch,
        compiler_params=pltpu.CompilerParams(
            collective_id=0, has_side_effects=True, vmem_limit_bytes=63 * 1024 * 1024
        ),
        cost_estimate=pl.CostEstimate(
            flops=12 * total * model * hid, bytes_accessed=8 * model * hid, transcendentals=half * hid
        ),
    )(tokens, up_latent, down_latent, out_grad)


def solution(mesh):
    in_specs = (P("col", "row"), P("row", "col"), P("col", "row"), P("col", "row"))
    out_specs = (P("col", "row"), P("col", "row"), P("row", "col"), P("col", "row"))
    return jax.shard_map(body, mesh=mesh, in_specs=in_specs, out_specs=out_specs, check_vma=False)
```
